512 devices in a mesh: tower: 2 (over core), seq: 64 (over y, x, z_hi), head: 4 (over z_lo).
Axes of the slice: x: 4, y: 4, z: 16 (z_hi: 4, z_lo: 4; z = z_hi * 4 + z_lo), core: 2. Of those that a mesh axis runs over, the one named last changes fastest.
Arguments:
- queries: bfloat16 [2, 4096, 3072], P('tower', ('seq', 'head')), may hold values from -100 to 100
- key_rows: bfloat16 [2, 4096, 3072], P('tower', ('seq', 'head')), may hold values from -4 to 4
- value_rows: bfloat16 [2, 4096, 3072], P('tower', ('seq', 'head')), may hold values from -6 to 6
- hidden: bfloat16 [2, 4096, 3072], P('tower', 'seq', 'head'), may hold values from -6 to 6
- gate_table: bfloat16 [2, 1000, 3072], P('tower', None, 'head'), may hold values from -8 to 8
- lengths: int32 [2, 1, 3], replicated, may hold values from 1 to 2048, 4096 in all within a row
- step_ids: int32 [1, 3], replicated, may hold values from 0 to 999
Outputs:
- mixed: bfloat16 [2, 4096, 3072], P('tower', 'seq', 'head')
The draws below stay inside these ranges and needn't reach their ends.
Inputs may be any that keep to these rules, and one draw needn't show every extreme that they name: Each row holds the lengths of the 3 samples of one pack in order and sums to 4096; its largest entry is 2048; sample k of a pack is the same clip in both towers.
All inputs are finite; a program needn't handle non-finite values.
Results may differ from the reference program's by a relative error of at most 0.0034.
Values may be sent and summed in bfloat16 or wider, within the bound.
No kernel may reach another device: no remote copies, remote signals or barrier semaphores. Data moves between devices by JAX's collectives and lax.ppermute only.
A program may use at most 128 MiB of HBM per device.

```python
import math
import jax
import jax.numpy as jnp
import numpy as np
from jax import lax

HEADS = 24
HEAD_DIM = 128
D = 3072
TOK_DEV = 64
PACK_SPAN = 64
SAMPLES = 3
NT = 1000
TOKENS = 4096
PACKS = 1


def shared_keys(key):
    return jax.random.truncated_normal(key, -4.0, 4.0, (2, TOKENS, D), jnp.float32)


def draw_queries(key, part):
    key = jax.random.fold_in(key, 1)
    values_drawn = 1.5 * jax.random.truncated_normal(key, -4.0, 4.0, (2, TOKENS, D), jnp.float32)
    return values_drawn.astype(jnp.bfloat16)


def draw_key_rows(key, part):
    shared = shared_keys(key)
    return shared.astype(jnp.bfloat16)


def block_scale(stream_key, extent, shards, least, top_value):
    gain = 1.0
    for axis_at, shards_of in shards:
        heights = jax.random.uniform(jax.random.fold_in(jax.random.fold_in(stream_key, 6), axis_at), (shards_of,), jnp.float32, least / len(shards), top_value / len(shards))
        gain = gain * jnp.repeat(jnp.exp(heights), extent[axis_at] // shards_of).reshape((-1,) + (1,) * (len(extent) - 1 - axis_at))
    return gain


def split_up(count, total, most, lean):
    portions = [(1 << 20) // math.isqrt(standing ** lean) + 1 for standing in range(2, count + 1)]
    surplus, holding = total - most - (count - 1), [1] * (count - 1)
    while surplus > 0:
        candidates = [i for i in range(count - 1) if holding[i] < most]
        mass, left = sum([portions[i] for i in candidates]), surplus
        for i in candidates:
            more = min(most - holding[i], max(1, left * portions[i] // mass), surplus)
            holding[i] = holding[i] + more
            surplus = surplus - more
    return np.array([most] + holding)


def uneven_parts(own_key, amount, total, reach, lean):
    if amount == 2:
        one = jax.random.randint(own_key, (), max(1, total - reach), min(reach, total - 1) + 1)
        return jnp.stack([one, total - one])
    sizes = jnp.asarray(split_up(amount, total, reach, lean), jnp.int32)
    couples = (amount - 1) // 2
    source_of, sink = sizes[1:1 + 2 * couples:2], sizes[2:2 + 2 * couples:2]
    room = jnp.minimum(source_of - 1, reach - sink)
    passed = jax.random.randint(jax.random.fold_in(own_key, 1), (couples,), 0, 1 << 20) % (room + 1)
    sizes = sizes.at[1:1 + 2 * couples:2].set(source_of - passed).at[2:2 + 2 * couples:2].set(sink + passed)
    return sizes[jax.random.permutation(jax.random.fold_in(own_key, 2), amount)]


def bell_draw(rng, dims, spread, limit, split=(), kind=jnp.bfloat16):
    entries = spread * jax.random.normal(rng, dims, jnp.float32)
    if split:
        entries = entries * block_scale(rng, dims, split, -0.22, 0.18)
    return jnp.clip(entries, -limit, limit).astype(kind)


def setup_inputs(seed: int = 0) -> dict:
    streams_of = jax.random.split(jax.random.key(seed), 8)
    queries = draw_queries(jax.random.fold_in(streams_of[7], 71), 0)
    key_rows = draw_key_rows(jax.random.fold_in(streams_of[7], 71), 0)
    value_rows = bell_draw(streams_of[2], (2, TOKENS, D), 1.0, 6.0, ((0, 2), (1, 256)))
    hidden = bell_draw(streams_of[3], (2, TOKENS, D), 1.0, 6.0, ((0, 2), (1, 64), (2, 4)))
    gate_table = bell_draw(streams_of[4], (2, NT, D), 2.0, 8.0, ((0, 2), (2, 4)))
    lengths = jax.vmap(lambda own: uneven_parts(own, SAMPLES, PACK_SPAN * TOK_DEV, PACK_SPAN * TOK_DEV // 2, 2))(jax.random.split(streams_of[5], 2 * PACKS)).reshape((2, PACKS, SAMPLES)).astype(jnp.int32)
    step_ids = jax.random.randint(streams_of[6], (PACKS, SAMPLES), 0, NT).astype(jnp.int32)
    return dict(queries=queries, key_rows=key_rows, value_rows=value_rows, hidden=hidden, gate_table=gate_table, lengths=lengths, step_ids=step_ids)


def sample_ids(positions, pack_lengths):
    bounds = jnp.cumsum(pack_lengths)[:-1]
    return jnp.sum((positions[:, None] >= bounds[None, :]).astype(jnp.int32), axis=1)


def reference(queries, key_rows, value_rows, hidden, gate_table, lengths, step_ids):
    span_rows = PACK_SPAN * TOK_DEV
    pack_total = TOKENS // span_rows
    positions = jnp.arange(span_rows, dtype=jnp.int32)
    score_scale = HEAD_DIM ** -0.5
    towers = []
    for tower_index in range(2):
        far_index = 1 - tower_index

        def one_pack(pack_index):
            first_row = (pack_index * span_rows).astype(jnp.int32)
            query_pack = lax.dynamic_slice_in_dim(queries[tower_index], first_row, span_rows, 0)
            key_pack = lax.dynamic_slice_in_dim(key_rows[far_index], first_row, span_rows, 0)
            value_pack = lax.dynamic_slice_in_dim(value_rows[far_index], first_row, span_rows, 0)
            query_ids = sample_ids(positions, lengths[tower_index][pack_index])
            key_ids = sample_ids(positions, lengths[far_index][pack_index])
            allowed = query_ids[:, None] == key_ids[None, :]

            def one_head(head_index):
                first_col = (head_index * HEAD_DIM).astype(jnp.int32)
                query_head = lax.dynamic_slice_in_dim(query_pack, first_col, HEAD_DIM, 1)
                key_head = lax.dynamic_slice_in_dim(key_pack, first_col, HEAD_DIM, 1)
                value_head = lax.dynamic_slice_in_dim(value_pack, first_col, HEAD_DIM, 1)
                scores = jnp.dot(query_head, key_head.T, preferred_element_type=jnp.float32) * score_scale
                scores = jnp.where(allowed, scores, -1e30)
                row_max = jnp.max(scores, axis=1, keepdims=True)
                expterm = jnp.exp(scores - row_max)
                weights = (expterm / jnp.sum(expterm, axis=1, keepdims=True)).astype(jnp.bfloat16)
                return jnp.dot(weights, value_head, preferred_element_type=jnp.float32)

            per_head = lax.map(one_head, jnp.arange(HEADS, dtype=jnp.int32))
            attended = jnp.moveaxis(per_head, 0, 1).reshape(span_rows, D)
            row_steps = step_ids[pack_index][query_ids]
            gate_rows = gate_table[tower_index][row_steps].astype(jnp.float32)
            residual_rows = lax.dynamic_slice_in_dim(hidden[tower_index], first_row, span_rows, 0).astype(jnp.float32)
            return (residual_rows + gate_rows * attended).astype(jnp.bfloat16)

        combined = lax.map(one_pack, jnp.arange(pack_total, dtype=jnp.int32))
        towers.append(combined.reshape(TOKENS, D))
    return jnp.stack(towers)
```

```python
import functools

import jax
import jax.numpy as jnp
from jax import lax
from jax.experimental import pallas as pl
from jax.experimental.pallas import tpu as pltpu
from jax.sharding import Mesh, PartitionSpec as P

HEAD_DIM = 128
SCALE = HEAD_DIM**-0.5 * 1.4426950408889634
MASKED = -(2.0**100)
COLUMNS = ("y", "x")
STATS = 128


def sample_of(positions, bound_a, bound_b):
    return (positions >= bound_a).astype(jnp.int32) + (positions >= bound_b).astype(jnp.int32)


def pack_kernel(q_ref, k_ref, v_ref, kv_ref, qs_ref):
    groups, rows, width = qs_ref.shape
    for g in range(groups):
        cols = slice(g * width, (g + 1) * width)
        qs_ref[g] = q_ref[0, :, cols]
        kv_ref[g, :rows] = k_ref[0, :, cols]
        kv_ref[g, rows:] = v_ref[0, :, cols]


def attend_kernel(info_ref, q_ref, *refs):
    kv_refs, out_ref = refs[:-1], refs[-1]
    columns, rows, width = q_ref.shape
    heads = width // HEAD_DIM
    chunks = len(kv_refs)
    sources, pair_rows, _ = kv_refs[0].shape
    part = pair_rows // 2
    per_chunk = sources * part
    keys = chunks * per_chunk
    own_a, own_b, far_a, far_b = (info_ref[i] for i in range(4))
    first_key, zhi = info_ref[4], info_ref[5]

    lane = lax.broadcasted_iota(jnp.int32, (1, keys), 1)
    key_at = first_key + lax.rem(lane // per_chunk + zhi, chunks) * per_chunk + lane % per_chunk
    key_ids = sample_of(key_at, far_a, far_b)
    stat_lane = lax.broadcasted_iota(jnp.int32, (1, STATS), 1)
    block = 4
    tile = block * rows

    def step(t, _):
        r = lax.broadcasted_iota(jnp.int32, (tile, 1), 0)
        query_at = ((t * block + r // rows) * chunks + zhi) * rows + r % rows
        allowed = sample_of(query_at, own_a, own_b) == key_ids
        stats = jnp.zeros((tile, STATS), jnp.float32)
        for h in range(heads):
            cols = slice(h * HEAD_DIM, (h + 1) * HEAD_DIM)
            q = q_ref[pl.ds(t * block, block), :, cols].reshape(tile, HEAD_DIM)
            k = jnp.concatenate(
                [ref[s, :part, cols] for ref in kv_refs for s in range(sources)], axis=0
            )
            v = jnp.concatenate(
                [ref[s, part:, cols] for ref in kv_refs for s in range(sources)], axis=0
            )
            v = jnp.concatenate([v, jnp.ones((keys, HEAD_DIM), v.dtype)], axis=1)
            s = lax.dot_general(q, k, (((1,), (1,)), ((), ())), preferred_element_type=jnp.float32)
            s = jnp.where(allowed, s * SCALE, MASKED)
            top = jnp.max(s, axis=1, keepdims=True).astype(jnp.bfloat16).astype(jnp.float32)
            p = jnp.exp2(s - top).astype(jnp.bfloat16)
            o = jnp.dot(p, v, preferred_element_type=jnp.float32)
            out_ref[pl.ds(t * block, block), :, cols] = (
                o[:, :HEAD_DIM].astype(jnp.bfloat16).reshape(block, rows, HEAD_DIM)
            )
            total = o[:, HEAD_DIM:]
            high = total.astype(jnp.bfloat16).astype(jnp.float32)
            stats = jnp.where(stat_lane == h, top, stats)
            stats = jnp.where(stat_lane == 32 + h, high, stats)
            stats = jnp.where(stat_lane == 64 + h, total - high, stats)
        out_ref[pl.ds(t * block, block), :, width:] = stats.astype(jnp.bfloat16).reshape(
            block, rows, STATS
        )
        return 0

    lax.fori_loop(0, columns // block, step, 0)


def merge_kernel(info_ref, parts_ref, hidden_ref, gates_ref, out_ref):
    columns, rows, full = parts_ref.shape
    width = full - STATS
    heads = width // HEAD_DIM
    own_a, own_b, first_row = info_ref[0], info_ref[1], info_ref[6]
    stats = [parts_ref[j, :, width:].astype(jnp.float32) for j in range(columns)]
    top = functools.reduce(jnp.maximum, stats)
    scales, total = [], jnp.zeros_like(top)
    for st in stats:
        scale = jnp.exp2(jnp.minimum(st - top, 0.0))
        sums = pltpu.roll(st, STATS - 32, 1) + pltpu.roll(st, STATS - 64, 1)
        scales.append(scale)
        total = total + scale * sums
    inverse = 1.0 / total
    scales = [scale * inverse for scale in scales]
    at = first_row + lax.broadcasted_iota(jnp.int32, (rows, 1), 0)
    ids = sample_of(at, own_a, own_b)
    for h in range(heads):
        cols = slice(h * HEAD_DIM, (h + 1) * HEAD_DIM)
        o = jnp.zeros((rows, HEAD_DIM), jnp.float32)
        for j in range(columns):
            o = o + scales[j][:, h : h + 1] * parts_ref[j, :, cols].astype(jnp.float32)
        gate = jnp.where(
            ids == 0,
            gates_ref[0:1, cols],
            jnp.where(ids == 1, gates_ref[1:2, cols], gates_ref[2:3, cols]),
        )
        out_ref[0, :, cols] = (hidden_ref[0, :, cols].astype(jnp.float32) + gate * o).astype(
            jnp.bfloat16
        )


def vmem(n):
    return [pl.BlockSpec(memory_space=pltpu.VMEM)] * n


SMEM = pl.BlockSpec(memory_space=pltpu.SMEM)
PARAMS = pltpu.CompilerParams(vmem_limit_bytes=40 * 1024 * 1024)


def shards(queries, key_rows, value_rows, hidden, gate_table, lengths, step_ids):
    groups = lax.axis_size("head")
    columns = lax.axis_size(COLUMNS)
    chunks = lax.axis_size("zhi")
    tower, zhi, column = lax.axis_index("tower"), lax.axis_index("zhi"), lax.axis_index(COLUMNS)
    rows, width = queries.shape[1], queries.shape[2] // groups
    own_rows = rows * groups

    kv, qs = pl.pallas_call(
        pack_kernel,
        out_shape=(
            jax.ShapeDtypeStruct((groups, 2 * rows, width), jnp.bfloat16),
            jax.ShapeDtypeStruct((groups, rows, width), jnp.bfloat16),
        ),
        in_specs=vmem(3),
        out_specs=tuple(vmem(2)),
        name="pack",
    )(queries, key_rows, value_rows)

    kv = lax.all_to_all(kv, "head", 0, 0, tiled=True)
    far = []
    for shift in range(chunks):
        route = [
            (t * chunks + (z + shift) % chunks, (1 - t) * chunks + z)
            for t in range(2)
            for z in range(chunks)
        ]
        far.append(lax.ppermute(kv, ("tower", "zhi"), route))

    qs = lax.all_to_all(qs, "head", 0, 0, tiled=True).reshape(own_rows, width)
    qs = jnp.broadcast_to(qs[None], (columns, own_rows, width))
    qs = lax.all_to_all(qs, COLUMNS, 0, 0, tiled=True)

    flat = lengths[:, 0, :]
    own = lax.dynamic_index_in_dim(flat, tower, 0, False)
    other = lax.dynamic_index_in_dim(flat, 1 - tower, 0, False)
    info = jnp.stack(
        [
            own[0],
            own[0] + own[1],
            other[0],
            other[0] + other[1],
            column * chunks * own_rows,
            zhi,
            (column * chunks + zhi) * own_rows,
            jnp.int32(0),
        ]
    ).astype(jnp.int32)
    wanted = jnp.zeros((8,), jnp.int32).at[:3].set(step_ids[0])
    selector = wanted[:, None] == jnp.arange(gate_table.shape[1], dtype=jnp.int32)[None, :]
    gates = jnp.dot(
        selector.astype(jnp.bfloat16), gate_table[0], preferred_element_type=jnp.float32
    )

    parts = pl.pallas_call(
        attend_kernel,
        out_shape=jax.ShapeDtypeStruct((columns, own_rows, width + STATS), jnp.bfloat16),
        in_specs=[SMEM] + vmem(1 + chunks),
        out_specs=vmem(1)[0],
        compiler_params=PARAMS,
        name="attend",
    )(info, qs, *far)
    parts = lax.all_to_all(parts, COLUMNS, 0, 0, tiled=True)
    return pl.pallas_call(
        merge_kernel,
        out_shape=jax.ShapeDtypeStruct(hidden.shape, jnp.bfloat16),
        in_specs=[SMEM] + vmem(3),
        out_specs=vmem(1)[0],
        compiler_params=PARAMS,
        name="merge",
    )(info, parts, hidden, gates)


def solution(mesh):
    towers, seq, head = mesh.devices.shape
    fine = Mesh(
        mesh.devices.reshape(towers, 4, 4, seq // 16, head), ("tower", "y", "x", "zhi", "head")
    )
    rows = P("tower", ("y", "x", "zhi", "head"), None)
    block = P("tower", ("y", "x", "zhi"), "head")
    return jax.shard_map(
        shards,
        mesh=fine,
        in_specs=(rows, rows, rows, block, P("tower", None, "head"), P(), P()),
        out_specs=block,
        check_vma=False,
    )
```

```python
import functools

import jax
import jax.numpy as jnp
from jax import lax
from jax.experimental import pallas as pl
from jax.experimental.pallas import tpu as pltpu
from jax.sharding import Mesh, PartitionSpec as P

HEAD_DIM = 128
SCALE = HEAD_DIM**-0.5 * 1.4426950408889634
MASKED = -(2.0**100)
STATS = 128
SPLIT = 2
COLUMNS = ("yl", "x")


def sample_of(positions, bound_a, bound_b):
    return (positions >= bound_a).astype(jnp.int32) + (positions >= bound_b).astype(jnp.int32)


def bounds(lengths_ref, tower):
    first = lengths_ref[tower, 0, 0]
    return first, first + lengths_ref[tower, 0, 1]


def position(yh, yl, x, zhi, row, rows):
    column = (yh * lax.axis_size("yl") + yl) * lax.axis_size("x") + x
    return (column * lax.axis_size("zhi") + zhi) * rows + row


def pack_kernel(q_ref, k_ref, v_ref, out_ref):
    pairs, both, width = out_ref.shape
    halves = lax.axis_size("yh")
    groups, rows = pairs // (2 * halves), both // 2
    mine = lax.axis_index("tower") * (halves * groups)
    other = halves * groups - mine
    for s in range(halves):
        for g in range(groups):
            cols = slice((g * halves + s) * width, (g * halves + s + 1) * width)
            at = s * groups + g
            out_ref[mine + at, :rows] = q_ref[0, :, cols]
            out_ref[mine + at, rows:] = jnp.zeros((rows, width), jnp.bfloat16)
            out_ref[other + at, :rows] = k_ref[0, :, cols]
            out_ref[other + at, rows:] = v_ref[0, :, cols]


def copies_kernel(in_ref, q_ref, kv_ref):
    pairs, both, _ = in_ref.shape
    sources, rows = pairs // 2, both // 2
    mine = lax.axis_index("tower") * sources
    other = sources - mine
    for g in range(sources):
        q = in_ref[mine + g, :rows]
        k = in_ref[other + g, :rows]
        v = in_ref[other + g, rows:]
        for c in range(q_ref.shape[0]):
            q_ref[c, g * rows : (g + 1) * rows] = q
        for c in range(kv_ref.shape[0]):
            kv_ref[c, g * rows : (g + 1) * rows] = k
            kv_ref[c, (sources + g) * rows : (sources + g + 1) * rows] = v


def attend_kernel(lengths_ref, q_ref, kv_ref, out_ref):
    columns, part, width = q_ref.shape
    chunks = kv_ref.shape[0]
    heads = width // HEAD_DIM
    halves = lax.axis_size("yh")
    rows = part // halves
    keys = chunks * part
    tower = lax.axis_index("tower")
    yl, x, zhi = lax.axis_index("yl"), lax.axis_index("x"), lax.axis_index("zhi")
    own_a, own_b = bounds(lengths_ref, tower)
    far_a, far_b = bounds(lengths_ref, 1 - tower)

    lane = lax.broadcasted_iota(jnp.int32, (1, keys), 1)
    within = lane % part
    key_at = position(within // rows, yl, x, lane // part, within % rows, rows)
    key_ids = sample_of(key_at, far_a, far_b)
    stat_lane = lax.broadcasted_iota(jnp.int32, (1, STATS), 1)
    block = 2
    tile = block * part

    def step(t, _):
        r = lax.broadcasted_iota(jnp.int32, (tile, 1), 0)
        column, within = t * block + r // part, r % part
        query_at = position(
            within // rows,
            column // lax.axis_size("x"),
            column % lax.axis_size("x"),
            zhi,
            within % rows,
            rows,
        )
        allowed = sample_of(query_at, own_a, own_b) == key_ids
        stats = jnp.zeros((tile, STATS), jnp.float32)
        for h in range(heads):
            cols = slice(h * HEAD_DIM, (h + 1) * HEAD_DIM)
            q = q_ref[pl.ds(t * block, block), :, cols].reshape(tile, HEAD_DIM)
            k = kv_ref[:, :part, cols].reshape(keys, HEAD_DIM)
            v = kv_ref[:, part:, cols].reshape(keys, HEAD_DIM)
            v = jnp.concatenate([v, jnp.ones((keys, HEAD_DIM), v.dtype)], axis=1)
            s = lax.dot_general(q, k, (((1,), (1,)), ((), ())), preferred_element_type=jnp.float32)
            s = jnp.where(allowed, s * SCALE, MASKED)
            top = jnp.max(s, axis=1, keepdims=True).astype(jnp.bfloat16).astype(jnp.float32)
            p = jnp.exp2(s - top).astype(jnp.bfloat16)
            o = jnp.dot(p, v, preferred_element_type=jnp.float32)
            total = o[:, HEAD_DIM:]
            high = total.astype(jnp.bfloat16).astype(jnp.float32)
            stats = jnp.where(stat_lane == h, top, stats)
            stats = jnp.where(stat_lane == 32 + h, high, stats)
            stats = jnp.where(stat_lane == 64 + h, total - high, stats)
            o = o[:, :HEAD_DIM].astype(jnp.bfloat16).reshape(block, halves, rows, HEAD_DIM)
            for s2 in range(halves):
                out_ref[s2, pl.ds(t * block, block), :, cols] = o[:, s2]
        stats = stats.astype(jnp.bfloat16).reshape(block, halves, rows, STATS)
        for s2 in range(halves):
            out_ref[s2, pl.ds(t * block, block), :, width:] = stats[:, s2]
        return 0

    lax.fori_loop(0, columns // block, step, 0)


def merge_kernel(lengths_ref, steps_ref, parts_ref, hidden_ref, table_ref, out_ref):
    halves, columns, rows, full = parts_ref.shape
    width = full - STATS
    heads = width // HEAD_DIM
    own_a, own_b = bounds(lengths_ref, lax.axis_index("tower"))
    yh, yl, x = lax.axis_index("yh"), lax.axis_index("yl"), lax.axis_index("x")
    row = lax.broadcasted_iota(jnp.int32, (rows, 1), 0)
    ids = sample_of(position(yh, yl, x, lax.axis_index("zhi"), row, rows), own_a, own_b)
    row_steps = jnp.where(
        ids == 0, steps_ref[0, 0], jnp.where(ids == 1, steps_ref[0, 1], steps_ref[0, 2])
    )
    chosen = row_steps == lax.broadcasted_iota(jnp.int32, (1, table_ref.shape[1]), 1)
    chosen = jnp.where(chosen, 1.0, 0.0).astype(jnp.bfloat16)
    gates = jnp.dot(chosen, table_ref[0], preferred_element_type=jnp.float32)
    for s2 in range(halves):
        stats = [parts_ref[s2, j, :, width:].astype(jnp.float32) for j in range(columns)]
        top = functools.reduce(jnp.maximum, stats)
        scales, total = [], jnp.zeros_like(top)
        for st in stats:
            scale = jnp.exp2(jnp.minimum(st - top, 0.0))
            sums = pltpu.roll(st, STATS - 32, 1) + pltpu.roll(st, STATS - 64, 1)
            scales.append(scale)
            total = total + scale * sums
        inverse = 1.0 / total
        scales = [scale * inverse for scale in scales]
        for h in range(heads):
            cols = slice(h * HEAD_DIM, (h + 1) * HEAD_DIM)
            o = jnp.zeros((rows, HEAD_DIM), jnp.float32)
            for j in range(columns):
                part = parts_ref[s2, j, :, cols].astype(jnp.float32)
                o = o + scales[j][:, h : h + 1] * part
            cols = slice(s2 * width + h * HEAD_DIM, s2 * width + (h + 1) * HEAD_DIM)
            out_ref[0, :, cols] = (
                hidden_ref[0, :, cols].astype(jnp.float32) + gates[:, cols] * o
            ).astype(jnp.bfloat16)


def vmem(n):
    return [pl.BlockSpec(memory_space=pltpu.VMEM)] * n


SMEM = pl.BlockSpec(memory_space=pltpu.SMEM)
PARAMS = pltpu.CompilerParams(vmem_limit_bytes=40 * 1024 * 1024)


def shards(queries, key_rows, value_rows, hidden, gate_table, lengths, step_ids):
    groups = lax.axis_size("head")
    halves = lax.axis_size("yh")
    columns = lax.axis_size(COLUMNS)
    chunks = lax.axis_size("zhi")
    rows, width = queries.shape[1], queries.shape[2] // (groups * halves)
    part = rows * groups * halves

    sent = pl.pallas_call(
        pack_kernel,
        out_shape=jax.ShapeDtypeStruct((2 * halves * groups, 2 * rows, width), jnp.bfloat16),
        in_specs=vmem(3),
        out_specs=vmem(1)[0],
        name="pack",
    )(queries, key_rows, value_rows)
    sent = lax.all_to_all(sent, ("tower", "yh", "head"), 0, 0, tiled=True)
    qs, kv = pl.pallas_call(
        copies_kernel,
        out_shape=(
            jax.ShapeDtypeStruct((columns, part, width), jnp.bfloat16),
            jax.ShapeDtypeStruct((1, 2 * part, width), jnp.bfloat16),
        ),
        in_specs=vmem(1),
        out_specs=tuple(vmem(2)),
        compiler_params=PARAMS,
        name="copies",
    )(sent)
    qs = lax.all_to_all(qs, COLUMNS, 0, 0, tiled=True)
    kv = lax.all_gather(kv[0], "zhi", axis=0, tiled=True).reshape(chunks, 2 * part, width)

    parts = pl.pallas_call(
        attend_kernel,
        out_shape=jax.ShapeDtypeStruct(
            (halves, columns, part // halves, width + STATS), jnp.bfloat16
        ),
        in_specs=[SMEM] + vmem(2),
        out_specs=vmem(1)[0],
        compiler_params=PARAMS,
        name="attend",
    )(lengths, qs, kv)
    parts, hidden, gate_table = lax.optimization_barrier((parts, hidden, gate_table))
    shape = parts.shape
    parts = lax.all_to_all(
        parts.reshape((halves * columns,) + shape[2:]), ("yh",) + COLUMNS, 0, 0, tiled=True
    )
    return pl.pallas_call(
        merge_kernel,
        out_shape=jax.ShapeDtypeStruct(hidden.shape, jnp.bfloat16),
        in_specs=[SMEM, SMEM] + vmem(3),
        out_specs=vmem(1)[0],
        compiler_params=PARAMS,
        name="merge",
    )(lengths, step_ids, parts.reshape(shape), hidden, gate_table)


def solution(mesh):
    towers, seq, head = mesh.devices.shape
    fine = Mesh(
        mesh.devices.reshape(towers, SPLIT, 4 // SPLIT, 4, seq // 16, head),
        ("tower", "yh", "yl", "x", "zhi", "head"),
    )
    seq_axes = ("yh", "yl", "x", "zhi")
    rows = P("tower", seq_axes + ("head",), None)
    block = P("tower", seq_axes, "head")
    return jax.shard_map(
        shards,
        mesh=fine,
        in_specs=(rows, rows, rows, block, P("tower", None, "head"), P(), P()),
        out_specs=block,
        check_vma=False,
    )
```

```python
import functools

import jax
import jax.numpy as jnp
from jax import lax
from jax.experimental import pallas as pl
from jax.experimental.pallas import tpu as pltpu
from jax.sharding import Mesh, PartitionSpec as P

HEAD_DIM = 128
SCALE = HEAD_DIM**-0.5 * 1.4426950408889634
MASKED = -(2.0**100)
STATS = 16
SPLIT = 2
COLUMNS = ("yl", "x")


def sample_of(positions, bound_a, bound_b):
    return (positions >= bound_a).astype(jnp.int32) + (positions >= bound_b).astype(jnp.int32)


def bounds(lengths_ref, tower):
    first = lengths_ref[tower, 0, 0]
    return first, first + lengths_ref[tower, 0, 1]


def position(yh, yl, x, zhi, row, rows):
    column = (yl * lax.axis_size("yh") + yh) * lax.axis_size("x") + x
    return (column * lax.axis_size("zhi") + zhi) * rows + row


def pack_kernel(q_ref, k_ref, v_ref, out_ref):
    pairs, triple, width = out_ref.shape
    halves = lax.axis_size("yh")
    groups, rows = pairs // halves, triple // 3
    for i, ref in enumerate((q_ref, k_ref, v_ref)):
        for s in range(halves):
            for g in range(groups):
                cols = slice((g * halves + s) * width, (g * halves + s + 1) * width)
                out_ref[s * groups + g, i * rows : (i + 1) * rows] = ref[0, :, cols]


def copies_kernel(in_ref, q_ref, kv_ref):
    sources, triple, _ = in_ref.shape[1:]
    rows = triple // 3
    mine = lax.axis_index("tower")
    other = 1 - mine
    for g in range(sources):
        q = in_ref[mine, g, :rows]
        for c in range(q_ref.shape[0]):
            q_ref[c, g * rows : (g + 1) * rows] = q
        kv_ref[g * rows : (g + 1) * rows] = in_ref[other, g, rows : 2 * rows]
        kv_ref[(sources + g) * rows : (sources + g + 1) * rows] = in_ref[other, g, 2 * rows :]


def attend_kernel(lengths_ref, q_ref, kv_ref, out_ref):
    columns, part, width = q_ref.shape
    chunks = kv_ref.shape[0]
    heads = width // HEAD_DIM
    halves = lax.axis_size("yh")
    rows = part // halves
    keys = chunks * part
    tower = lax.axis_index("tower")
    yl, x, zhi = lax.axis_index("yl"), lax.axis_index("x"), lax.axis_index("zhi")
    own_a, own_b = bounds(lengths_ref, tower)
    far_a, far_b = bounds(lengths_ref, 1 - tower)

    lane = lax.broadcasted_iota(jnp.int32, (1, keys), 1)
    within = lane % part
    key_ids = sample_of(
        position(within // rows, yl, x, lane // part, within % rows, rows), far_a, far_b
    )
    lane = lax.broadcasted_iota(jnp.int32, (1, HEAD_DIM), 1)
    block = columns
    tile = block * part

    def step(t, _):
        r = lax.broadcasted_iota(jnp.int32, (tile, 1), 0)
        column, within = t * block + r // part, r % part
        query_at = position(
            within // rows,
            column // lax.axis_size("x"),
            column % lax.axis_size("x"),
            zhi,
            within % rows,
            rows,
        )
        allowed = sample_of(query_at, own_a, own_b) == key_ids
        stats = jnp.zeros((tile, HEAD_DIM), jnp.float32)
        for h in range(heads):
            cols = slice(h * HEAD_DIM, (h + 1) * HEAD_DIM)
            q = q_ref[pl.ds(t * block, block), :, cols].reshape(tile, HEAD_DIM)
            k = kv_ref[:, :part, cols].reshape(keys, HEAD_DIM)
            v = kv_ref[:, part:, cols].reshape(keys, HEAD_DIM)
            s = lax.dot_general(q, k, (((1,), (1,)), ((), ())), preferred_element_type=jnp.float32)
            s = jnp.where(allowed, s, MASKED)
            top = (jnp.max(s, axis=1, keepdims=True) * SCALE).astype(jnp.bfloat16)
            top = top.astype(jnp.float32)
            empty = top < 0.01 * MASKED
            shift = jnp.where(empty, 0.0, top)
            p = jnp.exp2(s * SCALE - shift)
            total = jnp.sum(p, axis=1, keepdims=True)
            o = jnp.dot(p.astype(jnp.bfloat16), v, preferred_element_type=jnp.float32)
            high = total.astype(jnp.bfloat16).astype(jnp.float32)
            stats = jnp.where(lane == h, jnp.where(empty, MASKED, top), stats)
            stats = jnp.where(lane == 4 + h, total - high, stats)
            stats = jnp.where(lane == 8 + h, high, stats)
            o = o.astype(jnp.bfloat16).reshape(block, halves, rows, HEAD_DIM)
            for s2 in range(halves):
                out_ref[s2, pl.ds(t * block, block), h * rows : (h + 1) * rows, :] = o[:, s2]
        pick = lax.broadcasted_iota(jnp.int32, (STATS, 1), 0) == lane
        stats = lax.dot_general(
            jnp.where(pick, 1.0, 0.0).astype(jnp.bfloat16),
            stats.astype(jnp.bfloat16),
            (((1,), (1,)), ((), ())),
            preferred_element_type=jnp.float32,
        ).astype(jnp.bfloat16)
        for c in range(block):
            for s2 in range(halves):
                at = (c * halves + s2) * rows
                out_ref[s2, t * block + c, heads * rows :, :rows] = stats[:, at : at + rows]
                out_ref[s2, t * block + c, heads * rows :, rows:] = jnp.zeros(
                    (STATS, HEAD_DIM - rows), jnp.bfloat16
                )
        return 0

    lax.fori_loop(0, columns // block, step, 0)


def merge_kernel(lengths_ref, steps_ref, parts_ref, hidden_ref, table_ref, out_ref):
    halves, columns, full, _ = parts_ref.shape
    rows = hidden_ref.shape[1]
    heads = (full - STATS) // rows
    own_a, own_b = bounds(lengths_ref, lax.axis_index("tower"))
    yh, yl, x = lax.axis_index("yh"), lax.axis_index("yl"), lax.axis_index("x")
    row = lax.broadcasted_iota(jnp.int32, (rows, 1), 0)
    ids = sample_of(position(yh, yl, x, lax.axis_index("zhi"), row, rows), own_a, own_b)

    gates = []
    for i in range(3):
        wanted = steps_ref[0, i]
        eight = table_ref[wanted // 8].astype(jnp.float32)
        found = lax.broadcasted_iota(jnp.int32, (8, 1), 0) == wanted % 8
        gates.append(jnp.sum(jnp.where(found, eight, 0.0), axis=0, keepdims=True))

    scales = []
    for s2 in range(halves):
        stats = [parts_ref[s2, j, heads * rows :, :].astype(jnp.float32) for j in range(columns)]
        tops = [st[:8] for st in stats]
        top = functools.reduce(jnp.maximum, tops)
        factors, total = [], jnp.zeros_like(top)
        for st in stats:
            factor = jnp.exp2(jnp.minimum(st[:8] - top, 0.0))
            sums = st[8:] + jnp.concatenate([st[4:8], st[:4]], axis=0)
            factors.append(factor)
            total = total + factor * sums
        inverse = 1.0 / jnp.where(total > 0.0, total, 1.0)
        scales += [factor * inverse for factor in factors]
    scales = jnp.concatenate(scales, axis=0).T
    for s2 in range(halves):
        for h in range(heads):
            o = jnp.zeros((rows, HEAD_DIM), jnp.float32)
            for j in range(columns):
                part = parts_ref[s2, j, h * rows : (h + 1) * rows, :].astype(jnp.float32)
                at = (s2 * columns + j) * 8 + h
                o = o + scales[:rows, at : at + 1] * part
            cols = slice((s2 * heads + h) * HEAD_DIM, (s2 * heads + h + 1) * HEAD_DIM)
            gate = jnp.where(
                ids == 0, gates[0][:, cols], jnp.where(ids == 1, gates[1][:, cols], gates[2][:, cols])
            )
            out_ref[0, :, cols] = (hidden_ref[0, :, cols].astype(jnp.float32) + gate * o).astype(
                jnp.bfloat16
            )


def vmem(n):
    return [pl.BlockSpec(memory_space=pltpu.VMEM)] * n


SMEM = pl.BlockSpec(memory_space=pltpu.SMEM)
HBM = pl.BlockSpec(memory_space=pltpu.HBM)


def params(mib):
    return pltpu.CompilerParams(vmem_limit_bytes=mib * 1024 * 1024)


def shards(queries, key_rows, value_rows, hidden, gate_table, lengths, step_ids):
    groups = lax.axis_size("head")
    halves = lax.axis_size("yh")
    columns = lax.axis_size(COLUMNS)
    chunks = lax.axis_size("zhi")
    rows, width = queries.shape[1], queries.shape[2] // (groups * halves)
    heads = width // HEAD_DIM
    part = rows * groups * halves

    sent = pl.pallas_call(
        pack_kernel,
        out_shape=jax.ShapeDtypeStruct((halves * groups, 3 * rows, width), jnp.bfloat16),
        in_specs=vmem(3),
        out_specs=vmem(1)[0],
        compiler_params=params(60),
        name="pack",
    )(queries, key_rows, value_rows)
    sent = lax.all_to_all(sent, ("yh", "head"), 0, 0, tiled=True)
    sent = lax.all_gather(sent, "tower", axis=0, tiled=False)
    qs, kv = pl.pallas_call(
        copies_kernel,
        out_shape=(
            jax.ShapeDtypeStruct((columns, part, width), jnp.bfloat16),
            jax.ShapeDtypeStruct((2 * part, width), jnp.bfloat16),
        ),
        in_specs=vmem(1),
        out_specs=tuple(vmem(2)),
        compiler_params=params(8),
        name="copies",
    )(sent)
    qs = lax.all_to_all(qs, COLUMNS, 0, 0, tiled=True)
    kv = lax.all_gather(kv, "zhi", axis=0, tiled=True).reshape(chunks, 2 * part, width)

    shape = (halves, columns, heads * (part // halves) + STATS, HEAD_DIM)
    parts = pl.pallas_call(
        attend_kernel,
        out_shape=jax.ShapeDtypeStruct(shape, jnp.bfloat16),
        in_specs=[SMEM] + vmem(2),
        out_specs=vmem(1)[0],
        compiler_params=params(24),
        name="attend",
    )(lengths, qs, kv)
    parts, hidden, gate_table = lax.optimization_barrier((parts, hidden, gate_table))
    parts = lax.all_to_all(
        parts.reshape((halves * columns,) + shape[2:]), ("yh",) + COLUMNS, 0, 0, tiled=True
    )
    return pl.pallas_call(
        merge_kernel,
        out_shape=jax.ShapeDtypeStruct(hidden.shape, jnp.bfloat16),
        in_specs=[SMEM, SMEM] + vmem(3),
        out_specs=vmem(1)[0],
        compiler_params=params(16),
        name="merge",
    )(
        lengths,
        step_ids,
        parts.reshape(shape),
        hidden,
        gate_table.reshape(gate_table.shape[1] // 8, 8, gate_table.shape[2]),
    )


def solution(mesh):
    towers, seq, head = mesh.devices.shape
    fine = Mesh(
        mesh.devices.reshape(towers, 4 // SPLIT, SPLIT, 4, seq // 16, head),
        ("tower", "yl", "yh", "x", "zhi", "head"),
    )
    seq_axes = ("yl", "yh", "x", "zhi")
    rows = P("tower", seq_axes + ("head",), None)
    block = P("tower", seq_axes, "head")
    return jax.shard_map(
        shards,
        mesh=fine,
        in_specs=(rows, rows, rows, block, P("tower", None, "head"), P(), P()),
        out_specs=block,
        check_vma=False,
    )
```

```python
import functools

import jax
import jax.numpy as jnp
from jax import lax
from jax.experimental import pallas as pl
from jax.experimental.pallas import tpu as pltpu
from jax.sharding import Mesh, PartitionSpec as P

HEAD_DIM = 128
SCALE = HEAD_DIM**-0.5 * 1.4426950408889634
MASKED = -(2.0**100)
STATS = 16
SPLIT = 2
COLUMNS = ("yl", "x")


def sample_of(positions, bound_a, bound_b):
    return (positions >= bound_a).astype(jnp.int32) + (positions >= bound_b).astype(jnp.int32)


def bounds(lengths_ref, tower):
    first = lengths_ref[tower, 0, 0]
    return first, first + lengths_ref[tower, 0, 1]


def position(yh, yl, x, zhi, row, rows):
    column = (yl * lax.axis_size("yh") + yh) * lax.axis_size("x") + x
    return (column * lax.axis_size("zhi") + zhi) * rows + row


def pack_kernel(steps_ref, q_ref, k_ref, v_ref, table_ref, out_ref, gates_ref, found, sems):
    fetches = [
        pltpu.make_async_copy(table_ref.at[steps_ref[0, i] // 8], found.at[i], sems.at[i])
        for i in range(3)
    ]
    for fetch in fetches:
        fetch.start()
    pairs, triple, width = out_ref.shape
    halves = lax.axis_size("yh")
    groups, rows = pairs // halves, triple // 3
    for i, ref in enumerate((q_ref, k_ref, v_ref)):
        for s in range(halves):
            for g in range(groups):
                cols = slice((g * halves + s) * width, (g * halves + s + 1) * width)
                out_ref[s * groups + g, i * rows : (i + 1) * rows] = ref[0, :, cols]
    gates_ref[...] = jnp.zeros(gates_ref.shape, jnp.float32)
    for i, fetch in enumerate(fetches):
        fetch.wait()
        wanted = lax.broadcasted_iota(jnp.int32, (8, 1), 0) == steps_ref[0, i] % 8
        row = jnp.where(wanted, found[i].astype(jnp.float32), 0.0)
        gates_ref[i : i + 1] = jnp.sum(row, axis=0, keepdims=True)


def copies_kernel(in_ref, q_ref, kv_ref):
    sources, triple, _ = in_ref.shape[1:]
    rows = triple // 3
    mine = lax.axis_index("tower")
    other = 1 - mine
    for g in range(sources):
        q = in_ref[mine, g, :rows]
        for c in range(q_ref.shape[0]):
            q_ref[c, g * rows : (g + 1) * rows] = q
        k = in_ref[other, g, rows : 2 * rows]
        v = in_ref[other, g, 2 * rows :]
        for c in range(kv_ref.shape[0]):
            kv_ref[c, g * rows : (g + 1) * rows] = k
            kv_ref[c, (sources + g) * rows : (sources + g + 1) * rows] = v


def place(over_z, i, within, rows):
    if over_z:
        yl, x, zhi = lax.axis_index("yl"), lax.axis_index("x"), i
    else:
        yl, x, zhi = i // lax.axis_size("x"), i % lax.axis_size("x"), lax.axis_index("zhi")
    return position(within // rows, yl, x, zhi, within % rows, rows)


def attend_kernel(keys_over_z, lengths_ref, q_ref, kv_ref, out_ref):
    blocks, part, width = q_ref.shape
    heads = width // HEAD_DIM
    halves = lax.axis_size("yh")
    rows = part // halves
    keys = kv_ref.shape[0] * part
    tile = blocks * part
    tower = lax.axis_index("tower")
    own_a, own_b = bounds(lengths_ref, tower)
    far_a, far_b = bounds(lengths_ref, 1 - tower)

    lane = lax.broadcasted_iota(jnp.int32, (1, keys), 1)
    key_ids = sample_of(place(keys_over_z, lane // part, lane % part, rows), far_a, far_b)
    r = lax.broadcasted_iota(jnp.int32, (tile, 1), 0)
    query_at = place(not keys_over_z, r // part, r % part, rows)
    lane = lax.broadcasted_iota(jnp.int32, (1, HEAD_DIM), 1)
    allowed = sample_of(query_at, own_a, own_b) == key_ids
    stats = jnp.zeros((tile, HEAD_DIM), jnp.float32)
    for h in range(heads):
        cols = slice(h * HEAD_DIM, (h + 1) * HEAD_DIM)
        q = q_ref[:, :, cols].reshape(tile, HEAD_DIM)
        k = kv_ref[:, :part, cols].reshape(keys, HEAD_DIM)
        v = kv_ref[:, part:, cols].reshape(keys, HEAD_DIM)
        s = lax.dot_general(q, k, (((1,), (1,)), ((), ())), preferred_element_type=jnp.float32)
        s = jnp.where(allowed, s, MASKED)
        top = (jnp.max(s, axis=1, keepdims=True) * SCALE).astype(jnp.bfloat16)
        top = top.astype(jnp.float32)
        empty = top < 0.01 * MASKED
        shift = jnp.where(empty, 0.0, top)
        p = jnp.exp2(s * SCALE - shift)
        total = jnp.sum(p, axis=1, keepdims=True)
        o = jnp.dot(p.astype(jnp.bfloat16), v, preferred_element_type=jnp.float32)
        high = total.astype(jnp.bfloat16).astype(jnp.float32)
        stats = jnp.where(lane == h, jnp.where(empty, MASKED, top), stats)
        stats = jnp.where(lane == 4 + h, total - high, stats)
        stats = jnp.where(lane == 8 + h, high, stats)
        o = o.astype(jnp.bfloat16).reshape(blocks, halves, rows, HEAD_DIM)
        for s2 in range(halves):
            out_ref[s2, :, h * rows : (h + 1) * rows, :] = o[:, s2]
    pick = lax.broadcasted_iota(jnp.int32, (STATS, 1), 0) == lane
    stats = lax.dot_general(
        jnp.where(pick, 1.0, 0.0).astype(jnp.bfloat16),
        stats.astype(jnp.bfloat16),
        (((1,), (1,)), ((), ())),
        preferred_element_type=jnp.float32,
    ).astype(jnp.bfloat16)
    for c in range(blocks):
        for s2 in range(halves):
            at = (c * halves + s2) * rows
            out_ref[s2, c, heads * rows :, :rows] = stats[:, at : at + rows]
            out_ref[s2, c, heads * rows :, rows:] = jnp.zeros(
                (STATS, HEAD_DIM - rows), jnp.bfloat16
            )


def merge_kernel(lengths_ref, parts_ref, hidden_ref, gates_ref, out_ref):
    halves, columns, full, _ = parts_ref.shape
    rows = hidden_ref.shape[1]
    heads = (full - STATS) // rows
    own_a, own_b = bounds(lengths_ref, lax.axis_index("tower"))
    yh, yl, x = lax.axis_index("yh"), lax.axis_index("yl"), lax.axis_index("x")
    row = lax.broadcasted_iota(jnp.int32, (rows, 1), 0)
    ids = sample_of(position(yh, yl, x, lax.axis_index("zhi"), row, rows), own_a, own_b)

    scales = []
    for s2 in range(halves):
        stats = [parts_ref[s2, j, heads * rows :, :].astype(jnp.float32) for j in range(columns)]
        tops = [st[:8] for st in stats]
        top = functools.reduce(jnp.maximum, tops)
        factors, total = [], jnp.zeros_like(top)
        for st in stats:
            factor = jnp.exp2(jnp.minimum(st[:8] - top, 0.0))
            sums = st[8:] + jnp.concatenate([st[4:8], st[:4]], axis=0)
            factors.append(factor)
            total = total + factor * sums
        inverse = 1.0 / jnp.where(total > 0.0, total, 1.0)
        scales += [factor * inverse for factor in factors]
    scales = jnp.concatenate(scales, axis=0).T
    for s2 in range(halves):
        for h in range(heads):
            o = jnp.zeros((rows, HEAD_DIM), jnp.float32)
            for j in range(columns):
                part = parts_ref[s2, j, h * rows : (h + 1) * rows, :].astype(jnp.float32)
                at = (s2 * columns + j) * 8 + h
                o = o + scales[:rows, at : at + 1] * part
            cols = slice((s2 * heads + h) * HEAD_DIM, (s2 * heads + h + 1) * HEAD_DIM)
            gate = jnp.where(
                ids == 0,
                gates_ref[0:1, cols],
                jnp.where(ids == 1, gates_ref[1:2, cols], gates_ref[2:3, cols]),
            )
            out_ref[0, :, cols] = (hidden_ref[0, :, cols].astype(jnp.float32) + gate * o).astype(
                jnp.bfloat16
            )


def vmem(n):
    return [pl.BlockSpec(memory_space=pltpu.VMEM)] * n


SMEM = pl.BlockSpec(memory_space=pltpu.SMEM)
HBM = pl.BlockSpec(memory_space=pltpu.HBM)


def params(mib):
    return pltpu.CompilerParams(vmem_limit_bytes=mib * 1024 * 1024)


def shards(queries, key_rows, value_rows, hidden, gate_table, lengths, step_ids):
    groups = lax.axis_size("head")
    halves = lax.axis_size("yh")
    columns = lax.axis_size(COLUMNS)
    chunks = lax.axis_size("zhi")
    rows, width = queries.shape[1], queries.shape[2] // (groups * halves)
    heads = width // HEAD_DIM
    part = rows * groups * halves

    table = gate_table.reshape(gate_table.shape[1] // 8, 8, gate_table.shape[2])
    sent, gates = pl.pallas_call(
        pack_kernel,
        out_shape=(
            jax.ShapeDtypeStruct((halves * groups, 3 * rows, width), jnp.bfloat16),
            jax.ShapeDtypeStruct((8, table.shape[2]), jnp.float32),
        ),
        in_specs=[SMEM] + vmem(3) + [HBM],
        out_specs=tuple(vmem(2)),
        scratch_shapes=[
            pltpu.VMEM((3,) + table.shape[1:], jnp.bfloat16),
            pltpu.SemaphoreType.DMA((3,)),
        ],
        compiler_params=params(60),
        name="pack",
    )(step_ids, queries, key_rows, value_rows, table)
    sent = lax.all_to_all(sent, ("yh", "head"), 0, 0, tiled=True)
    sent = lax.all_gather(sent, "tower", axis=0, tiled=False)
    def finish(keys_over_z, back, qs, kv, hidden, gates):
        shape = (halves, qs.shape[0], heads * (part // halves) + STATS, HEAD_DIM)
        parts = pl.pallas_call(
            functools.partial(attend_kernel, keys_over_z),
            out_shape=jax.ShapeDtypeStruct(shape, jnp.bfloat16),
            in_specs=[SMEM] + vmem(2),
            out_specs=vmem(1)[0],
            compiler_params=params(24),
            name="attend",
        )(lengths, qs, kv)
        parts, hidden, gates = lax.optimization_barrier((parts, hidden, gates))
        parts = lax.all_to_all(
            parts.reshape((shape[0] * shape[1],) + shape[2:]), ("yh",) + back, 0, 0, tiled=True
        )
        return pl.pallas_call(
            merge_kernel,
            out_shape=jax.ShapeDtypeStruct(hidden.shape, jnp.bfloat16),
            in_specs=[SMEM] + vmem(3),
            out_specs=vmem(1)[0],
            compiler_params=params(16),
            name="merge",
        )(lengths, parts.reshape(shape), hidden, gates)

    def split(sent, query_copies, key_copies):
        return pl.pallas_call(
            copies_kernel,
            out_shape=(
                jax.ShapeDtypeStruct((query_copies, part, width), jnp.bfloat16),
                jax.ShapeDtypeStruct((key_copies, 2 * part, width), jnp.bfloat16),
            ),
            in_specs=vmem(1),
            out_specs=tuple(vmem(2)),
            compiler_params=params(8),
            name="copies",
        )(sent)

    def keys_beside(sent, hidden, gates):
        qs, kv = split(sent, columns, 1)
        qs = lax.all_to_all(qs, COLUMNS, 0, 0, tiled=True)
        kv = lax.all_gather(kv[0], "zhi", axis=0, tiled=True).reshape(chunks, 2 * part, width)
        return finish(True, COLUMNS, qs, kv, hidden, gates)

    def keys_first(sent, hidden, gates):
        qs, kv = split(sent, columns, 1)
        kv = lax.all_gather(kv[0], "zhi", axis=0, tiled=True).reshape(chunks, 2 * part, width)
        qs, kv = lax.optimization_barrier((qs, kv))
        qs = lax.all_to_all(qs, COLUMNS, 0, 0, tiled=True)
        return finish(True, COLUMNS, qs, kv, hidden, gates)

    def queries_beside(sent, hidden, gates):
        qs, kv = split(sent, 1, columns)
        kv = lax.all_to_all(kv, COLUMNS, 0, 0, tiled=True)
        qs = lax.all_gather(qs[0], "zhi", axis=0, tiled=True).reshape(chunks, part, width)
        return finish(False, ("zhi",), qs, kv, hidden, gates)

    plane = lax.axis_index("head")
    which = ((plane == 0) + 2 * (plane == 2) + 2 * (plane == 3)).astype(jnp.int32)
    return lax.switch(which, [keys_first, keys_beside, queries_beside], sent, hidden, gates)


def solution(mesh):
    towers, seq, head = mesh.devices.shape
    fine = Mesh(
        mesh.devices.reshape(towers, 4 // SPLIT, SPLIT, 4, seq // 16, head),
        ("tower", "yl", "yh", "x", "zhi", "head"),
    )
    seq_axes = ("yl", "yh", "x", "zhi")
    rows = P("tower", seq_axes + ("head",), None)
    block = P("tower", seq_axes, "head")
    return jax.shard_map(
        shards,
        mesh=fine,
        in_specs=(rows, rows, rows, block, P("tower", None, "head"), P(), P()),
        out_specs=block,
        check_vma=False,
    )
```

```python
import functools

import jax
import jax.numpy as jnp
from jax import lax
from jax.experimental import pallas as pl
from jax.experimental.pallas import tpu as pltpu
from jax.sharding import Mesh, PartitionSpec as P

HEAD_DIM = 128
SCALE = HEAD_DIM**-0.5 * 1.4426950408889634
MASKED = -(2.0**100)
STATS = 16
SPLIT = 2
COLUMNS = ("yl", "x")


def sample_of(positions, bound_a, bound_b):
    return (positions >= bound_a).astype(jnp.int32) + (positions >= bound_b).astype(jnp.int32)


def bounds(lengths_ref, tower):
    first = lengths_ref[tower, 0, 0]
    return first, first + lengths_ref[tower, 0, 1]


def position(yh, yl, x, zhi, row, rows):
    column = (yl * lax.axis_size("yh") + yh) * lax.axis_size("x") + x
    return (column * lax.axis_size("zhi") + zhi) * rows + row


def pack_kernel(q_ref, k_ref, v_ref, out_ref):
    pairs, triple, width = out_ref.shape
    halves = lax.axis_size("yh")
    groups, rows = pairs // halves, triple // 3
    for i, ref in enumerate((q_ref, k_ref, v_ref)):
        for s in range(halves):
            for g in range(groups):
                cols = slice((g * halves + s) * width, (g * halves + s + 1) * width)
                out_ref[s * groups + g, i * rows : (i + 1) * rows] = ref[0, :, cols]


def gates_kernel(steps_ref, table_ref, gates_ref, found, sems):
    fetches = [
        pltpu.make_async_copy(table_ref.at[steps_ref[0, i] // 8], found.at[i], sems.at[i])
        for i in range(3)
    ]
    for fetch in fetches:
        fetch.start()
    gates_ref[...] = jnp.zeros(gates_ref.shape, jnp.float32)
    for i, fetch in enumerate(fetches):
        fetch.wait()
        wanted = lax.broadcasted_iota(jnp.int32, (8, 1), 0) == steps_ref[0, i] % 8
        row = jnp.where(wanted, found[i].astype(jnp.float32), 0.0)
        gates_ref[i : i + 1] = jnp.sum(row, axis=0, keepdims=True)


def copies_kernel(in_ref, q_ref, kv_ref):
    sources, triple, _ = in_ref.shape[1:]
    rows = triple // 3
    mine = lax.axis_index("tower")
    other = 1 - mine
    for g in range(sources):
        q = in_ref[mine, g, :rows]
        for c in range(q_ref.shape[0]):
            q_ref[c, g * rows : (g + 1) * rows] = q
        k = in_ref[other, g, rows : 2 * rows]
        v = in_ref[other, g, 2 * rows :]
        for c in range(kv_ref.shape[0]):
            kv_ref[c, g * rows : (g + 1) * rows] = k
            kv_ref[c, (sources + g) * rows : (sources + g + 1) * rows] = v


def place(over_z, i, within, rows):
    if over_z:
        yl, x, zhi = lax.axis_index("yl"), lax.axis_index("x"), i
    else:
        yl, x, zhi = i // lax.axis_size("x"), i % lax.axis_size("x"), lax.axis_index("zhi")
    return position(within // rows, yl, x, zhi, within % rows, rows)


def attend_kernel(keys_over_z, lengths_ref, q_ref, kv_ref, out_ref):
    blocks, part, width = q_ref.shape
    heads = width // HEAD_DIM
    halves = lax.axis_size("yh")
    rows = part // halves
    keys = kv_ref.shape[0] * part
    tile = blocks * part
    tower = lax.axis_index("tower")
    own_a, own_b = bounds(lengths_ref, tower)
    far_a, far_b = bounds(lengths_ref, 1 - tower)

    lane = lax.broadcasted_iota(jnp.int32, (1, keys), 1)
    key_ids = sample_of(place(keys_over_z, lane // part, lane % part, rows), far_a, far_b)
    r = lax.broadcasted_iota(jnp.int32, (tile, 1), 0)
    query_at = place(not keys_over_z, r // part, r % part, rows)
    lane = lax.broadcasted_iota(jnp.int32, (1, HEAD_DIM), 1)
    allowed = sample_of(query_at, own_a, own_b) == key_ids
    stats = jnp.zeros((tile, HEAD_DIM), jnp.float32)
    for h in range(heads):
        cols = slice(h * HEAD_DIM, (h + 1) * HEAD_DIM)
        q = q_ref[:, :, cols].reshape(tile, HEAD_DIM)
        k = kv_ref[:, :part, cols].reshape(keys, HEAD_DIM)
        v = kv_ref[:, part:, cols].reshape(keys, HEAD_DIM)
        s = lax.dot_general(q, k, (((1,), (1,)), ((), ())), preferred_element_type=jnp.float32)
        s = jnp.where(allowed, s, MASKED)
        top = (jnp.max(s, axis=1, keepdims=True) * SCALE).astype(jnp.bfloat16)
        top = top.astype(jnp.float32)
        empty = top < 0.01 * MASKED
        shift = jnp.where(empty, 0.0, top)
        p = jnp.exp2(s * SCALE - shift)
        total = jnp.sum(p, axis=1, keepdims=True)
        o = jnp.dot(p.astype(jnp.bfloat16), v, preferred_element_type=jnp.float32)
        high = total.astype(jnp.bfloat16).astype(jnp.float32)
        stats = jnp.where(lane == h, jnp.where(empty, MASKED, top), stats)
        stats = jnp.where(lane == 4 + h, total - high, stats)
        stats = jnp.where(lane == 8 + h, high, stats)
        o = o.astype(jnp.bfloat16).reshape(blocks, halves, rows, HEAD_DIM)
        for s2 in range(halves):
            out_ref[s2, :, h * rows : (h + 1) * rows, :] = o[:, s2]
    pick = lax.broadcasted_iota(jnp.int32, (STATS, 1), 0) == lane
    stats = lax.dot_general(
        jnp.where(pick, 1.0, 0.0).astype(jnp.bfloat16),
        stats.astype(jnp.bfloat16),
        (((1,), (1,)), ((), ())),
        preferred_element_type=jnp.float32,
    ).astype(jnp.bfloat16)
    for c in range(blocks):
        for s2 in range(halves):
            at = (c * halves + s2) * rows
            out_ref[s2, c, heads * rows :, :rows] = stats[:, at : at + rows]
            out_ref[s2, c, heads * rows :, rows:] = jnp.zeros(
                (STATS, HEAD_DIM - rows), jnp.bfloat16
            )


def merge_kernel(lengths_ref, parts_ref, hidden_ref, gates_ref, out_ref):
    halves, columns, full, _ = parts_ref.shape
    rows = hidden_ref.shape[1]
    heads = (full - STATS) // rows
    own_a, own_b = bounds(lengths_ref, lax.axis_index("tower"))
    yh, yl, x = lax.axis_index("yh"), lax.axis_index("yl"), lax.axis_index("x")
    row = lax.broadcasted_iota(jnp.int32, (rows, 1), 0)
    ids = sample_of(position(yh, yl, x, lax.axis_index("zhi"), row, rows), own_a, own_b)

    scales = []
    for s2 in range(halves):
        stats = [parts_ref[s2, j, heads * rows :, :].astype(jnp.float32) for j in range(columns)]
        tops = [st[:8] for st in stats]
        top = functools.reduce(jnp.maximum, tops)
        factors, total = [], jnp.zeros_like(top)
        for st in stats:
            factor = jnp.exp2(jnp.minimum(st[:8] - top, 0.0))
            sums = st[8:] + jnp.concatenate([st[4:8], st[:4]], axis=0)
            factors.append(factor)
            total = total + factor * sums
        inverse = 1.0 / jnp.where(total > 0.0, total, 1.0)
        scales += [factor * inverse for factor in factors]
    scales = jnp.concatenate(scales, axis=0).T
    for s2 in range(halves):
        for h in range(heads):
            o = jnp.zeros((rows, HEAD_DIM), jnp.float32)
            for j in range(columns):
                part = parts_ref[s2, j, h * rows : (h + 1) * rows, :].astype(jnp.float32)
                at = (s2 * columns + j) * 8 + h
                o = o + scales[:rows, at : at + 1] * part
            cols = slice((s2 * heads + h) * HEAD_DIM, (s2 * heads + h + 1) * HEAD_DIM)
            gate = jnp.where(
                ids == 0,
                gates_ref[0:1, cols],
                jnp.where(ids == 1, gates_ref[1:2, cols], gates_ref[2:3, cols]),
            )
            out_ref[0, :, cols] = (hidden_ref[0, :, cols].astype(jnp.float32) + gate * o).astype(
                jnp.bfloat16
            )


def vmem(n):
    return [pl.BlockSpec(memory_space=pltpu.VMEM)] * n


SMEM = pl.BlockSpec(memory_space=pltpu.SMEM)
HBM = pl.BlockSpec(memory_space=pltpu.HBM)


def params(mib):
    return pltpu.CompilerParams(vmem_limit_bytes=mib * 1024 * 1024)


def shards(queries, key_rows, value_rows, hidden, gate_table, lengths, step_ids):
    groups = lax.axis_size("head")
    halves = lax.axis_size("yh")
    columns = lax.axis_size(COLUMNS)
    chunks = lax.axis_size("zhi")
    rows, width = queries.shape[1], queries.shape[2] // (groups * halves)
    heads = width // HEAD_DIM
    part = rows * groups * halves

    sent = pl.pallas_call(
        pack_kernel,
        out_shape=jax.ShapeDtypeStruct((halves * groups, 3 * rows, width), jnp.bfloat16),
        in_specs=vmem(3),
        out_specs=vmem(1)[0],
        compiler_params=params(60),
        name="pack",
    )(queries, key_rows, value_rows)
    table = gate_table.reshape(gate_table.shape[1] // 8, 8, gate_table.shape[2])
    gates = pl.pallas_call(
        gates_kernel,
        out_shape=jax.ShapeDtypeStruct((8, table.shape[2]), jnp.float32),
        in_specs=[SMEM, HBM],
        out_specs=vmem(1)[0],
        scratch_shapes=[
            pltpu.VMEM((3,) + table.shape[1:], jnp.bfloat16),
            pltpu.SemaphoreType.DMA((3,)),
        ],
        compiler_params=params(60),
        cost_estimate=pl.CostEstimate(flops=100000, bytes_accessed=100000, transcendentals=0),
        name="gates",
    )(step_ids, table)
    sent = lax.all_to_all(sent, ("yh", "head"), 0, 0, tiled=True)
    sent = lax.all_gather(sent, "tower", axis=0, tiled=False)
    def finish(keys_over_z, back, qs, kv, hidden, gates):
        shape = (halves, qs.shape[0], heads * (part // halves) + STATS, HEAD_DIM)
        parts = pl.pallas_call(
            functools.partial(attend_kernel, keys_over_z),
            out_shape=jax.ShapeDtypeStruct(shape, jnp.bfloat16),
            in_specs=[SMEM] + vmem(2),
            out_specs=vmem(1)[0],
            compiler_params=params(24),
            name="attend",
        )(lengths, qs, kv)
        parts, hidden, gates = lax.optimization_barrier((parts, hidden, gates))
        parts = lax.all_to_all(
            parts.reshape((shape[0] * shape[1],) + shape[2:]), ("yh",) + back, 0, 0, tiled=True
        )
        return pl.pallas_call(
            merge_kernel,
            out_shape=jax.ShapeDtypeStruct(hidden.shape, jnp.bfloat16),
            in_specs=[SMEM] + vmem(3),
            out_specs=vmem(1)[0],
            compiler_params=params(16),
            name="merge",
        )(lengths, parts.reshape(shape), hidden, gates)

    def split(sent, query_copies, key_copies):
        return pl.pallas_call(
            copies_kernel,
            out_shape=(
                jax.ShapeDtypeStruct((query_copies, part, width), jnp.bfloat16),
                jax.ShapeDtypeStruct((key_copies, 2 * part, width), jnp.bfloat16),
            ),
            in_specs=vmem(1),
            out_specs=tuple(vmem(2)),
            compiler_params=params(8),
            name="copies",
        )(sent)

    def keys_beside(sent, hidden, gates):
        qs, kv = split(sent, columns, 1)
        qs = lax.all_to_all(qs, COLUMNS, 0, 0, tiled=True)
        kv = lax.all_gather(kv[0], "zhi", axis=0, tiled=True).reshape(chunks, 2 * part, width)
        return finish(True, COLUMNS, qs, kv, hidden, gates)

    def keys_first(sent, hidden, gates):
        qs, kv = split(sent, columns, 1)
        kv = lax.all_gather(kv[0], "zhi", axis=0, tiled=True).reshape(chunks, 2 * part, width)
        qs, kv = lax.optimization_barrier((qs, kv))
        qs = lax.all_to_all(qs, COLUMNS, 0, 0, tiled=True)
        return finish(True, COLUMNS, qs, kv, hidden, gates)

    def queries_beside(sent, hidden, gates):
        qs, kv = split(sent, 1, columns)
        kv = lax.all_to_all(kv, COLUMNS, 0, 0, tiled=True)
        qs = lax.all_gather(qs[0], "zhi", axis=0, tiled=True).reshape(chunks, part, width)
        return finish(False, ("zhi",), qs, kv, hidden, gates)

    plane = lax.axis_index("head")
    which = ((plane == 0) + 2 * (plane == 2) + 2 * (plane == 3)).astype(jnp.int32)
    return lax.switch(which, [keys_first, keys_beside, queries_beside], sent, hidden, gates)


def solution(mesh):
    towers, seq, head = mesh.devices.shape
    fine = Mesh(
        mesh.devices.reshape(towers, 4 // SPLIT, SPLIT, 4, seq // 16, head),
        ("tower", "yl", "yh", "x", "zhi", "head"),
    )
    seq_axes = ("yl", "yh", "x", "zhi")
    rows = P("tower", seq_axes + ("head",), None)
    block = P("tower", seq_axes, "head")
    return jax.shard_map(
        shards,
        mesh=fine,
        in_specs=(rows, rows, rows, block, P("tower", None, "head"), P(), P()),
        out_specs=block,
        check_vma=False,
    )
```

```python
import functools

import jax
import jax.numpy as jnp
from jax import lax
from jax.experimental import pallas as pl
from jax.experimental.pallas import tpu as pltpu
from jax.sharding import Mesh, PartitionSpec as P

HEAD_DIM = 128
SCALE = HEAD_DIM**-0.5 * 1.4426950408889634
MASKED = -(2.0**100)
STATS = 16
SPLIT = 2
COLUMNS = ("yl", "x")


def sample_of(positions, bound_a, bound_b):
    return (positions >= bound_a).astype(jnp.int32) + (positions >= bound_b).astype(jnp.int32)


def bounds(lengths_ref, tower):
    first = lengths_ref[tower, 0, 0]
    return first, first + lengths_ref[tower, 0, 1]


def position(yh, yl, x, zhi, row, rows):
    column = (yl * lax.axis_size("yh") + yh) * lax.axis_size("x") + x
    return (column * lax.axis_size("zhi") + zhi) * rows + row


def pack_kernel(q_ref, k_ref, v_ref, out_ref):
    pairs, triple, width = out_ref.shape
    halves = lax.axis_size("yh")
    groups, rows = pairs // halves, triple // 3
    for i, ref in enumerate((q_ref, k_ref, v_ref)):
        for s in range(halves):
            for g in range(groups):
                cols = slice((g * halves + s) * width, (g * halves + s + 1) * width)
                out_ref[s * groups + g, i * rows : (i + 1) * rows] = ref[0, :, cols]


def gates_kernel(steps_ref, table_ref, gates_ref, found, sems):
    fetches = [
        pltpu.make_async_copy(table_ref.at[steps_ref[0, i] // 8], found.at[i], sems.at[i])
        for i in range(3)
    ]
    for fetch in fetches:
        fetch.start()
    gates_ref[...] = jnp.zeros(gates_ref.shape, jnp.float32)
    for i, fetch in enumerate(fetches):
        fetch.wait()
        wanted = lax.broadcasted_iota(jnp.int32, (8, 1), 0) == steps_ref[0, i] % 8
        row = jnp.where(wanted, found[i].astype(jnp.float32), 0.0)
        gates_ref[i : i + 1] = jnp.sum(row, axis=0, keepdims=True)


def copies_kernel(in_ref, q_ref, kv_ref):
    sources, triple, _ = in_ref.shape[1:]
    rows = triple // 3
    mine = lax.axis_index("tower")
    other = 1 - mine
    for g in range(sources):
        q = in_ref[mine, g, :rows]
        for c in range(q_ref.shape[0]):
            q_ref[c, g * rows : (g + 1) * rows] = q
        k = in_ref[other, g, rows : 2 * rows]
        v = in_ref[other, g, 2 * rows :]
        for c in range(kv_ref.shape[0]):
            kv_ref[c, g * rows : (g + 1) * rows] = k
            kv_ref[c, (sources + g) * rows : (sources + g + 1) * rows] = v


def place(over_z, i, within, rows):
    if over_z:
        yl, x, zhi = lax.axis_index("yl"), lax.axis_index("x"), i
    else:
        yl, x, zhi = i // lax.axis_size("x"), i % lax.axis_size("x"), lax.axis_index("zhi")
    return position(within // rows, yl, x, zhi, within % rows, rows)


def attend_kernel(keys_over_z, lengths_ref, q_ref, kv_ref, out_ref):
    blocks, part, width = q_ref.shape
    heads = width // HEAD_DIM
    halves = lax.axis_size("yh")
    rows = part // halves
    keys = kv_ref.shape[0] * part
    tile = blocks * part
    tower = lax.axis_index("tower")
    own_a, own_b = bounds(lengths_ref, tower)
    far_a, far_b = bounds(lengths_ref, 1 - tower)

    lane = lax.broadcasted_iota(jnp.int32, (1, keys), 1)
    key_ids = sample_of(place(keys_over_z, lane // part, lane % part, rows), far_a, far_b)
    r = lax.broadcasted_iota(jnp.int32, (tile, 1), 0)
    query_at = place(not keys_over_z, r // part, r % part, rows)
    lane = lax.broadcasted_iota(jnp.int32, (1, HEAD_DIM), 1)
    allowed = sample_of(query_at, own_a, own_b) == key_ids
    stats = jnp.zeros((tile, HEAD_DIM), jnp.float32)
    for h in range(heads):
        cols = slice(h * HEAD_DIM, (h + 1) * HEAD_DIM)
        q = q_ref[:, :, cols].reshape(tile, HEAD_DIM)
        k = kv_ref[:, :part, cols].reshape(keys, HEAD_DIM)
        v = kv_ref[:, part:, cols].reshape(keys, HEAD_DIM)
        s = lax.dot_general(q, k, (((1,), (1,)), ((), ())), preferred_element_type=jnp.float32)
        s = jnp.where(allowed, s, MASKED)
        top = (jnp.max(s, axis=1, keepdims=True) * SCALE).astype(jnp.bfloat16)
        top = top.astype(jnp.float32)
        empty = top < 0.01 * MASKED
        shift = jnp.where(empty, 0.0, top)
        p = jnp.exp2(s * SCALE - shift)
        total = jnp.sum(p, axis=1, keepdims=True)
        o = jnp.dot(p.astype(jnp.bfloat16), v, preferred_element_type=jnp.float32)
        high = total.astype(jnp.bfloat16).astype(jnp.float32)
        stats = jnp.where(lane == h, jnp.where(empty, MASKED, top), stats)
        stats = jnp.where(lane == 4 + h, total - high, stats)
        stats = jnp.where(lane == 8 + h, high, stats)
        o = o.astype(jnp.bfloat16).reshape(blocks, halves, rows, HEAD_DIM)
        for s2 in range(halves):
            out_ref[s2, :, h * rows : (h + 1) * rows, :] = o[:, s2]
    pick = lax.broadcasted_iota(jnp.int32, (STATS, 1), 0) == lane
    stats = lax.dot_general(
        jnp.where(pick, 1.0, 0.0).astype(jnp.bfloat16),
        stats.astype(jnp.bfloat16),
        (((1,), (1,)), ((), ())),
        preferred_element_type=jnp.float32,
    ).astype(jnp.bfloat16)
    for c in range(blocks):
        for s2 in range(halves):
            at = (c * halves + s2) * rows
            out_ref[s2, c, heads * rows :, :rows] = stats[:, at : at + rows]
            out_ref[s2, c, heads * rows :, rows:] = jnp.zeros(
                (STATS, HEAD_DIM - rows), jnp.bfloat16
            )


def merge_kernel(lengths_ref, parts_ref, hidden_ref, gates_ref, out_ref):
    halves, columns, full, _ = parts_ref.shape
    rows = hidden_ref.shape[1]
    heads = (full - STATS) // rows
    own_a, own_b = bounds(lengths_ref, lax.axis_index("tower"))
    yh, yl, x = lax.axis_index("yh"), lax.axis_index("yl"), lax.axis_index("x")
    row = lax.broadcasted_iota(jnp.int32, (rows, 1), 0)
    ids = sample_of(position(yh, yl, x, lax.axis_index("zhi"), row, rows), own_a, own_b)

    scales = []
    for s2 in range(halves):
        stats = [parts_ref[s2, j, heads * rows :, :].astype(jnp.float32) for j in range(columns)]
        tops = [st[:8] for st in stats]
        top = functools.reduce(jnp.maximum, tops)
        factors, total = [], jnp.zeros_like(top)
        for st in stats:
            factor = jnp.exp2(jnp.minimum(st[:8] - top, 0.0))
            sums = st[8:] + jnp.concatenate([st[4:8], st[:4]], axis=0)
            factors.append(factor)
            total = total + factor * sums
        inverse = 1.0 / jnp.where(total > 0.0, total, 1.0)
        scales += [factor * inverse for factor in factors]
    scales = jnp.concatenate(scales, axis=0).T
    for s2 in range(halves):
        for h in range(heads):
            o = jnp.zeros((rows, HEAD_DIM), jnp.float32)
            for j in range(columns):
                part = parts_ref[s2, j, h * rows : (h + 1) * rows, :].astype(jnp.float32)
                at = (s2 * columns + j) * 8 + h
                o = o + scales[:rows, at : at + 1] * part
            cols = slice((s2 * heads + h) * HEAD_DIM, (s2 * heads + h + 1) * HEAD_DIM)
            gate = jnp.where(
                ids == 0,
                gates_ref[0:1, cols],
                jnp.where(ids == 1, gates_ref[1:2, cols], gates_ref[2:3, cols]),
            )
            out_ref[0, :, cols] = (hidden_ref[0, :, cols].astype(jnp.float32) + gate * o).astype(
                jnp.bfloat16
            )


def vmem(n):
    return [pl.BlockSpec(memory_space=pltpu.VMEM)] * n


SMEM = pl.BlockSpec(memory_space=pltpu.SMEM)
HBM = pl.BlockSpec(memory_space=pltpu.HBM)


def params(mib):
    return pltpu.CompilerParams(vmem_limit_bytes=mib * 1024 * 1024)


def shards(queries, key_rows, value_rows, hidden, gate_table, lengths, step_ids):
    groups = lax.axis_size("head")
    halves = lax.axis_size("yh")
    columns = lax.axis_size(COLUMNS)
    chunks = lax.axis_size("zhi")
    rows, width = queries.shape[1], queries.shape[2] // (groups * halves)
    heads = width // HEAD_DIM
    part = rows * groups * halves

    sent = pl.pallas_call(
        pack_kernel,
        out_shape=jax.ShapeDtypeStruct((halves * groups, 3 * rows, width), jnp.bfloat16),
        in_specs=vmem(3),
        out_specs=vmem(1)[0],
        compiler_params=params(60),
        name="pack",
    )(queries, key_rows, value_rows)
    table = gate_table.reshape(gate_table.shape[1] // 8, 8, gate_table.shape[2])
    gates = pl.pallas_call(
        gates_kernel,
        out_shape=jax.ShapeDtypeStruct((8, table.shape[2]), jnp.float32),
        in_specs=[SMEM, HBM],
        out_specs=vmem(1)[0],
        scratch_shapes=[
            pltpu.VMEM((3,) + table.shape[1:], jnp.bfloat16),
            pltpu.SemaphoreType.DMA((3,)),
        ],
        compiler_params=params(60),
        cost_estimate=pl.CostEstimate(flops=100000, bytes_accessed=100000, transcendentals=0),
        name="gates",
    )(step_ids, table)
    sent = lax.all_to_all(sent, ("yh", "head"), 0, 0, tiled=True)
    sent = lax.all_gather(sent, "tower", axis=0, tiled=False)
    def finish(keys_over_z, back, qs, kv, hidden, gates):
        shape = (halves, qs.shape[0], heads * (part // halves) + STATS, HEAD_DIM)
        parts = pl.pallas_call(
            functools.partial(attend_kernel, keys_over_z),
            out_shape=jax.ShapeDtypeStruct(shape, jnp.bfloat16),
            in_specs=[SMEM] + vmem(2),
            out_specs=vmem(1)[0],
            compiler_params=params(24),
            name="attend",
        )(lengths, qs, kv)
        parts, hidden, gates = lax.optimization_barrier((parts, hidden, gates))
        parts = lax.all_to_all(
            parts.reshape((shape[0] * shape[1],) + shape[2:]), ("yh",) + back, 0, 0, tiled=True
        )
        return pl.pallas_call(
            merge_kernel,
            out_shape=jax.ShapeDtypeStruct(hidden.shape, jnp.bfloat16),
            in_specs=[SMEM] + vmem(3),
            out_specs=vmem(1)[0],
            compiler_params=params(16),
            name="merge",
        )(lengths, parts.reshape(shape), hidden, gates)

    def split(sent, query_copies, key_copies):
        return pl.pallas_call(
            copies_kernel,
            out_shape=(
                jax.ShapeDtypeStruct((query_copies, part, width), jnp.bfloat16),
                jax.ShapeDtypeStruct((key_copies, 2 * part, width), jnp.bfloat16),
            ),
            in_specs=vmem(1),
            out_specs=tuple(vmem(2)),
            compiler_params=params(8),
            name="copies",
        )(sent)

    def keys_beside(sent, hidden, gates):
        qs, kv = split(sent, columns, 1)
        qs = lax.all_to_all(qs, COLUMNS, 0, 0, tiled=True)
        kv = lax.all_gather(kv[0], "zhi", axis=0, tiled=True).reshape(chunks, 2 * part, width)
        return finish(True, COLUMNS, qs, kv, hidden, gates)

    def keys_first(sent, hidden, gates):
        qs, kv = split(sent, 1, 1)
        kv = lax.all_gather(kv[0], "zhi", axis=0, tiled=True).reshape(chunks, 2 * part, width)
        qs, kv = lax.optimization_barrier((qs, kv))
        qs = jnp.broadcast_to(qs, (columns,) + qs.shape[1:])
        qs = lax.all_to_all(qs, COLUMNS, 0, 0, tiled=True)
        return finish(True, COLUMNS, qs, kv, hidden, gates)

    def queries_beside(sent, hidden, gates):
        qs, kv = split(sent, 1, columns)
        kv = lax.all_to_all(kv, COLUMNS, 0, 0, tiled=True)
        qs = lax.all_gather(qs[0], "zhi", axis=0, tiled=True).reshape(chunks, part, width)
        return finish(False, ("zhi",), qs, kv, hidden, gates)

    plane = lax.axis_index("head")
    which = ((plane == 0) + 2 * (plane == 2) + 2 * (plane == 3)).astype(jnp.int32)
    return lax.switch(which, [keys_first, keys_beside, queries_beside], sent, hidden, gates)


def solution(mesh):
    towers, seq, head = mesh.devices.shape
    fine = Mesh(
        mesh.devices.reshape(towers, 4 // SPLIT, SPLIT, 4, seq // 16, head),
        ("tower", "yl", "yh", "x", "zhi", "head"),
    )
    seq_axes = ("yl", "yh", "x", "zhi")
    rows = P("tower", seq_axes + ("head",), None)
    block = P("tower", seq_axes, "head")
    return jax.shard_map(
        shards,
        mesh=fine,
        in_specs=(rows, rows, rows, block, P("tower", None, "head"), P(), P()),
        out_specs=block,
        check_vma=False,
    )
```
